32 devices in a mesh: leaf: 8 (over z, x), obs: 4 (over y, core).
Axes of the slice: x: 2, y: 2, z: 4, core: 2. Of those that a mesh axis runs over, the one named last changes fastest.
Arguments:
- samples_z: bfloat16 [64, 2048], P('obs', 'leaf'), may hold values from -6 to 6
- diag_block: bfloat16 [2048, 256], P('leaf'), as said below
- level_basis: bfloat16 [3, 64, 2048], P(None, None, 'leaf'), may hold values from -6 to 6
- site_xy: float32 [2, 2048], P(None, 'leaf'), may hold values from 0 to 1, as said below
- obs_site: int32 [1024], P('leaf'), may hold values from 0 to 255
- obs_value: float32 [1024], P('leaf'), may hold values from -6 to 6
- obs_count: int32 [8], P('leaf'), may hold values from 1 to 128, 512 in all
- inverse_rows: float32 [512, 512], P(('leaf', 'obs')), may hold values from -0.0078125 to 0.0078125
Outputs:
- conditional: float32 [64, 2048], P('obs', 'leaf')
The draws below stay inside these ranges and needn't reach their ends.
Inputs may be any that keep to these rules, and one draw needn't show every extreme that they name: `obs_count`: each leaf block's count of observations; the counts sum to 512 and the largest is exactly 128. `obs_site`: slots at or past a block's count are not used. `diag_block`: each leaf block is symmetric. `site_xy`: coordinates lie in the unit square; the sites of each leaf block lie in one cell of a recursive halving of the square that follows the tree of blocks.
All inputs are finite; a program needn't handle non-finite values.
Results may differ from the reference program's by a relative error of at most 0.0003.
Values sent between devices are 32-bit elements; how exact they have to be, the bound alone decides.
A program may use at most 64 MiB of HBM per device.

```python
import math
import jax
import jax.numpy as jnp
import numpy as np
from jax import lax

NB = 256
S = 64
R = 64
OCAP = 128
LEVELS = 3
NSITES = 2048
M = 512
SLOTS = 1024
N_LEAF = 8


def draw_site_xy(key, part):
    index = jnp.arange(NSITES, dtype=jnp.int32)
    block = index // NB
    column = jnp.zeros((NSITES,), jnp.int32)
    row = jnp.zeros((NSITES,), jnp.int32)
    for level in range(LEVELS):
        digit = block >> level & 1
        if level % 2 == 0:
            column = column + (digit << level // 2)
        else:
            row = row + (digit << level // 2)
    columns = 2 ** ((LEVELS + 1) // 2)
    rows = 2 ** (LEVELS // 2)
    jitter = jax.random.uniform(key, (2, NSITES), jnp.float32)
    coord_x = (column.astype(jnp.float32) + jitter[0]) / columns
    coord_y = (row.astype(jnp.float32) + jitter[1]) / rows
    return jnp.stack([coord_x, coord_y], axis=0).astype(jnp.float32)


def draw_diag_block(key, part):
    raw = jax.random.normal(key, (N_LEAF, NB, NB), jnp.float32)
    paired = (raw + jnp.swapaxes(raw, 1, 2)) * (1.0 / jnp.sqrt(jnp.float32(2 * NB)))
    return paired.reshape(N_LEAF * NB, NB).astype(jnp.bfloat16)


def place_ends(values, rng, low, top_value):
    dims = values.shape
    place = [jax.random.randint(jax.random.fold_in(rng, axis), (), 0, dims[axis]) for axis in range(len(dims))]
    values = values.at[tuple(place)].set(low)
    longest = dims.index(max(dims))
    place[longest] = (place[longest] + 1) % dims[longest]
    return values.at[tuple(place)].set(top_value)


def steps_of(rng, extent, split, smallest, high):
    gain, own = 1.0, jax.random.fold_in(rng, 6)
    for axis_at, shards_of in split:
        steps = jnp.exp(jax.random.uniform(jax.random.fold_in(own, axis_at), (shards_of,), jnp.float32, smallest / len(split), high / len(split)))
        gain = gain * jnp.repeat(steps, extent[axis_at] // shards_of).reshape([-1 if axis == axis_at else 1 for axis in range(len(extent))])
    return gain


def profile(amount, total, reach, slope):
    portions = [(1 << 20) // math.isqrt(rank ** slope) + 1 for rank in range(2, amount + 1)]
    spare, given = total - reach - (amount - 1), [1] * (amount - 1)
    while spare > 0:
        candidates = [i for i in range(amount - 1) if given[i] < reach]
        whole, left = sum([portions[i] for i in candidates]), spare
        for i in candidates:
            more = min(reach - given[i], max(1, left * portions[i] // whole), spare)
            given[i] = given[i] + more
            spare = spare - more
    return np.array([reach] + given)


def ragged(key, amount, total, most, skew):
    if amount == 2:
        one = jax.random.randint(key, (), max(1, total - most), min(most, total - 1) + 1)
        return jnp.stack([one, total - one])
    sizes = jnp.asarray(profile(amount, total, most, skew), jnp.int32)
    pairs = (amount - 1) // 2
    source_of, taker = sizes[1:1 + 2 * pairs:2], sizes[2:2 + 2 * pairs:2]
    margin = jnp.minimum(source_of - 1, most - taker)
    moved = jax.random.randint(jax.random.fold_in(key, 1), (pairs,), 0, 1 << 20) % (margin + 1)
    sizes = sizes.at[1:1 + 2 * pairs:2].set(source_of - moved).at[2:2 + 2 * pairs:2].set(taker + moved)
    return sizes[jax.random.permutation(jax.random.fold_in(key, 2), amount)]


def gaussian(own_key, extent, scale, most, pieces=(), held_as=jnp.bfloat16):
    factor_of = steps_of(own_key, extent, pieces, -0.22, 0.18) if pieces else 1.0
    result = jax.random.normal(own_key, extent, jnp.float32) * scale * factor_of
    return jnp.minimum(jnp.maximum(result, -most), most).astype(held_as)


def setup_inputs(seed: int = 0) -> dict:
    keys = jax.random.split(jax.random.key(seed), 9)
    return {
        "samples_z": gaussian(keys[0], (S, NSITES), 1.0, 6.0, ((0, 4), (1, 8))),
        "diag_block": draw_diag_block(jax.random.fold_in(keys[8], 71), 0),
        "level_basis": gaussian(keys[2], (LEVELS, R, NSITES), 1.0, 6.0, ((2, 8),)),
        "site_xy": draw_site_xy(jax.random.fold_in(keys[8], 71), 0),
        "obs_site": place_ends(jax.random.randint(keys[4], (SLOTS,), 0, NB), jax.random.fold_in(keys[4], 1), 0, NB - 1).astype(jnp.int32),
        "obs_value": gaussian(keys[5], (SLOTS,), 1.0, 6.0, ((0, 8),), jnp.float32),
        "obs_count": ragged(keys[6], N_LEAF, M, OCAP, 2).astype(jnp.int32),
        "inverse_rows": gaussian(keys[7], (M, M), (M * 1024) ** -0.5, 0.0078125, ((0, 32),), jnp.float32),
    }


corr_length = 0.15

def compact_index(counts, slot_count, total):
    inclusive = jnp.cumsum(counts).astype(jnp.int32)
    number = jnp.arange(total, dtype=jnp.int32)
    passed = (inclusive[None, :] <= number[:, None]).astype(jnp.int32)
    owner = lax.optimization_barrier(jnp.sum(passed, axis=1)).astype(jnp.int32)
    base = lax.optimization_barrier(jnp.sum(passed * counts[None, :], axis=1)).astype(jnp.int32)
    return (owner * slot_count + number - base).astype(jnp.int32)

def kernel_tile(obs_xy, block_xy):
    delta_x = obs_xy[0][:, None] - block_xy[0][None, :]
    delta_y = obs_xy[1][:, None] - block_xy[1][None, :]
    distance = jnp.sqrt(delta_x * delta_x + delta_y * delta_y)
    return jnp.exp(-distance / corr_length)

def reference(samples_z, diag_block, level_basis, site_xy, obs_site, obs_value, obs_count, inverse_rows):
    draws = samples_z.astype(jnp.float32).reshape(S, N_LEAF, NB)
    blocks = diag_block.astype(jnp.float32).reshape(N_LEAF, NB, NB)
    field_diag = jnp.einsum('spn,pnm->spm', draws, blocks, precision=lax.Precision.HIGHEST)
    basis = level_basis.astype(jnp.float32).reshape(LEVELS, R, N_LEAF, NB)
    project = jnp.einsum('spn,lrpn->pslr', draws, basis, precision=lax.Precision.HIGHEST)
    coef_list = []
    for level in range(LEVELS):
        width = 2 ** level
        grouped = project[:, :, level, :].reshape(N_LEAF // (2 * width), 2, width, S, R)
        sums = lax.optimization_barrier(jnp.sum(grouped, axis=2))
        sibling = sums[:, ::-1]
        spread = jnp.broadcast_to(sibling[:, :, None], (N_LEAF // (2 * width), 2, width, S, R)).reshape(N_LEAF, S, R)
        factor = 0.5 / jnp.sqrt(jnp.float32(R * width * NB))
        coef_list.append(spread * factor)
    coefficients = jnp.stack(coef_list, axis=2)
    field_low = jnp.einsum('pslr,lrpn->spn', coefficients, basis, precision=lax.Precision.HIGHEST)
    field = (field_diag + field_low).reshape(S, NSITES)
    obs_index = compact_index(obs_count, OCAP, M)
    owner = (obs_index // OCAP).astype(jnp.int32)
    global_site = (owner * NB + obs_site[obs_index]).astype(jnp.int32)
    residual = obs_value[obs_index][None, :] - field[:, global_site]
    coef = lax.dot_general(residual, inverse_rows, (((1,), (1,)), ((), ())), precision=lax.Precision.HIGHEST, preferred_element_type=jnp.float32)
    obs_xy = site_xy[:, global_site]
    block_xy = site_xy.reshape(2, N_LEAF, NB).transpose(1, 0, 2)

    def one_block(xy_block):
        tile = kernel_tile(obs_xy, xy_block)
        return jnp.dot(coef, tile, precision=lax.Precision.HIGHEST, preferred_element_type=jnp.float32)
    correction = lax.map(one_block, block_xy)
    correction = correction.transpose(1, 0, 2).reshape(S, NSITES)
    return field + correction
```

```python
import functools

import jax
import jax.numpy as jnp
from jax import lax
from jax.experimental import pallas as pl
from jax.experimental.pallas import tpu as pltpu
from jax.sharding import PartitionSpec as P

corr_length = 0.15
MESH = pl.DeviceIdType.MESH
NT = (((1,), (1,)), ((), ()))
UNROLL = 8
CHUNK = 512
MSG = 16


def dot(a, b):
    return jnp.dot(a, b, preferred_element_type=jnp.float32)


def dot_nt(a, b):
    return lax.dot_general(a, b, NT, preferred_element_type=jnp.float32)


def split(a):
    high = a.astype(jnp.bfloat16)
    return high, (a - high.astype(jnp.float32)).astype(jnp.bfloat16)


def stacked(a):
    high, low = split(a)
    return jnp.concatenate([high, low], axis=0)


def loop(count, step):
    if count <= UNROLL:
        for i in range(count):
            step(i)
    else:

        def one(i, carry):
            step(i)
            return carry

        lax.fori_loop(0, count, one, 0)


def at(start, size):
    start = start if isinstance(start, int) else pl.multiple_of(start, size)
    return pl.ds(start, size)


def kernel(
    leaves,
    groups,
    z_ref,
    diag_ref,
    basis_ref,
    xy_ref,
    site_ref,
    value_ref,
    count_ref,
    inv_ref,
    out_ref,
    proj,
    abuf,
    mbuf,
    ibuf,
    rbuf,
    cbuf,
    xbuf,
    sbuf,
    kh,
    kl,
    slot_of,
    a_send,
    a_recv,
    m_send,
    m_recv,
    i_send,
    i_recv,
    r_send,
    r_recv,
    c_send,
    c_recv,
):
    p = lax.axis_index("leaf")
    o = lax.axis_index("obs")
    levels, rank, sites = basis_ref.shape
    samples = z_ref.shape[0]
    slots = site_ref.shape[1]
    rows = inv_ref.shape[0]
    total = inv_ref.shape[1]
    owned = rows * groups

    def partners(step):
        for level in reversed(range(levels)):
            width = 2**level
            half = p // width
            start = (half + 1 - 2 * (half % 2)) * width
            loop(width, functools.partial(lambda level, start, i: step(level, start + i), level, start))

    def peers(step):
        for e in range(1, groups):
            step((o + e) % groups)

    barrier = pltpu.get_barrier_semaphore()

    def greet(leaf, obs):
        pl.semaphore_signal(barrier, inc=1, device_id=(leaf, obs), device_id_type=MESH)

    partners(lambda level, q: greet(q, o))
    peers(lambda g: greet(p, g))

    def to_leaf(src, dst, send, recv, q, who):
        return pltpu.make_async_remote_copy(
            src_ref=src, dst_ref=dst, send_sem=send.at[q], recv_sem=recv.at[who],
            device_id=(q, o), device_id_type=MESH,
        )

    def a_copy(level, q, who):
        return to_leaf(proj.at[level], abuf.at[who], a_send, a_recv, q, who)

    def m_copy(q, who):
        return to_leaf(mbuf.at[who], mbuf.at[who], m_send, m_recv, q, who)

    def r_copy(q, who):
        part = rbuf.at[:, at(who * slots, slots)]
        return to_leaf(part, part, r_send, r_recv, q, who)

    def c_copy(q, who):
        return to_leaf(cbuf.at[who], cbuf.at[who], c_send, c_recv, q, who)

    def i_copy(g, who):
        part = ibuf.at[at(who * rows, rows), :]
        return pltpu.make_async_remote_copy(
            src_ref=part, dst_ref=part, send_sem=i_send.at[g], recv_sem=i_recv.at[who],
            device_id=(p, g), device_id_type=MESH,
        )

    z = z_ref[...]
    for level in range(levels):
        proj[level] = dot_nt(z, basis_ref[level])
    pick = (lax.broadcasted_iota(jnp.int32, (sites, slots), 0) == site_ref[...]).astype(jnp.float32)
    pick = pick.astype(jnp.bfloat16)
    row = lax.broadcasted_iota(jnp.int32, (MSG, sites), 0)
    coord = jnp.where(row < 3, xy_ref[0:1, :], xy_ref[1:2, :])
    first = coord.astype(jnp.bfloat16).astype(jnp.float32)
    second = (coord - first).astype(jnp.bfloat16).astype(jnp.float32)
    third = coord - first - second
    part = jnp.where(row % 3 == 0, first, jnp.where(row % 3 == 1, second, third))
    part = jnp.where(row < 6, part, 0.0).astype(jnp.bfloat16)
    message = dot(part, pick)
    count = count_ref[0].astype(jnp.float32)
    message = jnp.where(lax.broadcasted_iota(jnp.int32, (MSG, slots), 0) == 6, count, message)
    mbuf[p] = message
    ibuf[at(o * rows, rows), :] = inv_ref[...]

    pl.semaphore_wait(barrier, leaves - 1 + groups - 1)

    partners(lambda level, q: a_copy(level, q, p).start())
    partners(lambda level, q: m_copy(q, p).start())
    peers(lambda g: i_copy(g, o).start())

    at_slots = value_ref[...] - dot(z, dot(diag_ref[...], pick).astype(jnp.bfloat16))
    picked = [dot(basis_ref[level], pick).astype(jnp.bfloat16) for level in range(levels)]
    field = dot(z, diag_ref[...])

    partners(lambda level, q: a_copy(level, q, q).wait_recv())
    coefs = []
    for level in range(levels):
        width = 2**level
        half = p // width
        start = (half + 1 - 2 * (half % 2)) * width
        sums = abuf[start]
        if width <= UNROLL:
            for i in range(1, width):
                sums = sums + abuf[start + i]
        else:
            sums = lax.fori_loop(1, width, lambda i, s, start=start: s + abuf[start + i], sums)
        coefs.append(stacked(sums * (0.5 / (rank * width * sites) ** 0.5)))
    low = dot(coefs[0], picked[0])
    for level in range(1, levels):
        low = low + dot(coefs[level], picked[level])
    rbuf[:, at(p * slots, slots)] = at_slots - (low[:samples] + low[samples:])
    partners(lambda level, q: r_copy(q, p).start())

    low = dot(coefs[0], basis_ref[0])
    for level in range(1, levels):
        low = low + dot(coefs[level], basis_ref[level])
    out_ref[...] = field + (low[:samples] + low[samples:])

    partners(lambda level, q: m_copy(q, q).wait_recv())
    counts = jnp.concatenate([mbuf[q, 6:7, :] for q in range(leaves)], axis=0)
    below = lax.broadcasted_iota(jnp.int32, (leaves, leaves), 1) < lax.broadcasted_iota(
        jnp.int32, (leaves, leaves), 0
    )
    base = dot(below.astype(jnp.float32).astype(jnp.bfloat16), counts.astype(jnp.bfloat16))
    lane = lax.broadcasted_iota(jnp.int32, (leaves, slots), 1).astype(jnp.float32)
    slot_of[...] = jnp.where(lane < counts, base + lane, -1.0)
    chunk = min(CHUNK, total)
    number = lax.broadcasted_iota(jnp.int32, (chunk, slots), 0).astype(jnp.float32)
    peers(lambda g: i_copy(g, g).wait_recv())

    def one_chunk(c):
        inverse = stacked(ibuf[:, at(c * chunk, chunk)])
        shift = number + jnp.float32(c * chunk) if isinstance(c, int) else number + (c * chunk).astype(jnp.float32)

        def one_leaf(q):
            here = jnp.where(shift == slot_of[pl.ds(q, 1), :], 1.0, 0.0).astype(jnp.bfloat16)
            wide = dot(inverse, here)
            wide = wide[:owned] + wide[owned:]
            lanes = at(q * slots, slots)
            if chunk == total:
                xbuf[:, lanes] = wide
            else:
                xbuf[:, lanes] += wide
            places = dot_nt(here, mbuf[q].astype(jnp.bfloat16))
            if isinstance(q, int) and q == 0:
                sbuf[...] = places
            else:
                sbuf[...] += places

        if leaves > UNROLL:
            sbuf[...] = jnp.zeros_like(sbuf)
        loop(leaves, one_leaf)
        places = sbuf[...]

        def column(i):
            return jnp.broadcast_to(places[:, i : i + 1], (chunk, sites))

        delta_x = (column(0) + column(1) + column(2)) - xy_ref[0:1, :]
        delta_y = (column(3) + column(4) + column(5)) - xy_ref[1:2, :]
        distance = jnp.sqrt(delta_x * delta_x + delta_y * delta_y)
        high, rest = split(jnp.exp(distance * (-1.0 / corr_length)))
        kh[at(c * chunk, chunk), :] = high
        kl[at(c * chunk, chunk), :] = rest

    if chunk < total:
        xbuf[...] = jnp.zeros_like(xbuf)
    loop(total // chunk, one_chunk)
    xh, xl = split(xbuf[...])

    partners(lambda level, q: r_copy(q, q).wait_recv())
    rh, rl = split(rbuf[...])
    both = dot_nt(jnp.concatenate([rh, rl], axis=0), xh)
    cbuf[p] = both[:samples] + both[samples:] + dot_nt(rh, xl)
    partners(lambda level, q: c_copy(q, p).start())

    def drain(level, q):
        a_copy(level, q, p).wait_send()
        m_copy(q, p).wait_send()
        r_copy(q, p).wait_send()

    partners(drain)
    peers(lambda g: i_copy(g, o).wait_send())
    partners(lambda level, q: c_copy(q, q).wait_recv())

    def correct(q):
        coef = stacked(cbuf[q])
        lines = at(q * owned, owned)
        twice = dot(coef, kh[lines, :])
        return twice[:samples] + twice[samples:] + dot(coef[:samples], kl[lines, :])

    if leaves <= UNROLL:
        total_sum = correct(0)
        for q in range(1, leaves):
            total_sum = total_sum + correct(q)
    else:
        total_sum = lax.fori_loop(1, leaves, lambda q, s: s + correct(q), correct(0))
    out_ref[...] += total_sum
    partners(lambda level, q: c_copy(q, p).wait_send())


def body(samples_z, diag_block, level_basis, site_xy, obs_site, obs_value, obs_count, inverse_rows):
    leaves = lax.axis_size("leaf")
    groups = lax.axis_size("obs")
    samples, sites = samples_z.shape
    levels, rank, _ = level_basis.shape
    slots = obs_site.shape[0]
    rows, total = inverse_rows.shape
    owned = rows * groups
    vmem = pl.BlockSpec(memory_space=pltpu.VMEM)
    smem = pl.BlockSpec(memory_space=pltpu.SMEM)
    f32, bf16 = jnp.float32, jnp.bfloat16
    leaf_sem = pltpu.SemaphoreType.DMA((leaves,))
    obs_sem = pltpu.SemaphoreType.DMA((groups,))
    return pl.pallas_call(
        functools.partial(kernel, leaves, groups),
        out_shape=jax.ShapeDtypeStruct((samples, sites), f32),
        in_specs=[vmem] * 6 + [smem, vmem],
        out_specs=vmem,
        scratch_shapes=[
            pltpu.VMEM((levels, samples, rank), f32),
            pltpu.VMEM((leaves, samples, rank), f32),
            pltpu.VMEM((leaves, MSG, slots), f32),
            pltpu.VMEM((owned, total), f32),
            pltpu.VMEM((samples, leaves * slots), f32),
            pltpu.VMEM((leaves, samples, owned), f32),
            pltpu.VMEM((owned, leaves * slots), f32),
            pltpu.VMEM((min(CHUNK, total), MSG), f32),
            pltpu.VMEM((total, sites), bf16),
            pltpu.VMEM((total, sites), bf16),
            pltpu.VMEM((leaves, slots), f32),
            leaf_sem, leaf_sem, leaf_sem, leaf_sem,
            obs_sem, obs_sem,
            leaf_sem, leaf_sem, leaf_sem, leaf_sem,
        ],
        compiler_params=pltpu.CompilerParams(
            collective_id=0, has_side_effects=True, vmem_limit_bytes=40 * 2**20
        ),
        cost_estimate=pl.CostEstimate(
            flops=2 * samples * sites * total * 4,
            bytes_accessed=4 * owned * total,
            transcendentals=2 * total * sites,
        ),
    )(
        samples_z,
        diag_block,
        level_basis,
        site_xy,
        obs_site.reshape(1, slots),
        obs_value.reshape(1, slots),
        obs_count,
        inverse_rows,
    )


def solution(mesh):
    in_specs = (
        P("obs", "leaf"),
        P("leaf", None),
        P(None, None, "leaf"),
        P(None, "leaf"),
        P("leaf"),
        P("leaf"),
        P("leaf"),
        P(("leaf", "obs"), None),
    )
    out_specs = P("obs", "leaf")
    return jax.shard_map(body, mesh=mesh, in_specs=in_specs, out_specs=out_specs, check_vma=False)
```

```python
import functools

import jax
import jax.numpy as jnp
from jax import lax
from jax.experimental import pallas as pl
from jax.experimental.pallas import tpu as pltpu
from jax.sharding import PartitionSpec as P

corr_length = 0.15
MESH = pl.DeviceIdType.MESH
NT = (((1,), (1,)), ((), ()))
UNROLL = 8
CHUNK = 512
MSG = 16


def dot(a, b):
    return jnp.dot(a, b, preferred_element_type=jnp.float32)


def dot_nt(a, b):
    return lax.dot_general(a, b, NT, preferred_element_type=jnp.float32)


def split(a):
    high = a.astype(jnp.bfloat16)
    return high, (a - high.astype(jnp.float32)).astype(jnp.bfloat16)


def stacked(a):
    high, low = split(a)
    return jnp.concatenate([high, low], axis=0)


def loop(count, step):
    if count <= UNROLL:
        for i in range(count):
            step(i)
    else:

        def one(i, carry):
            step(i)
            return carry

        lax.fori_loop(0, count, one, 0)


def at(start, size):
    start = start if isinstance(start, int) else pl.multiple_of(start, size)
    return pl.ds(start, size)


def kernel(
    leaves,
    groups,
    z_hbm,
    diag_hbm,
    basis_hbm,
    xy_hbm,
    site_hbm,
    value_hbm,
    count_hbm,
    inv_hbm,
    out_ref,
    z_ref,
    diag_ref,
    basis_ref,
    xy_ref,
    site_ref,
    value_ref,
    count_ref,
    in_sem,
    proj,
    abuf,
    mbuf,
    ibuf,
    rbuf,
    cbuf,
    xbuf,
    sbuf,
    kh,
    kl,
    slot_of,
    a_send,
    a_recv,
    m_send,
    m_recv,
    i_send,
    i_recv,
    r_send,
    r_recv,
    c_send,
    c_recv,
):
    p = lax.axis_index("leaf")
    o = lax.axis_index("obs")
    levels, rank, sites = basis_ref.shape
    samples = z_ref.shape[0]
    slots = site_ref.shape[1]
    rows, total = inv_hbm.shape
    owned = rows * groups

    def partners(step):
        for level in reversed(range(levels)):
            width = 2**level
            half = p // width
            start = (half + 1 - 2 * (half % 2)) * width
            loop(width, functools.partial(lambda level, start, i: step(level, start + i), level, start))

    def peers(step):
        for e in range(1, groups):
            step((o + e) % groups)

    own_rows = ibuf.at[at(o * rows, rows), :]
    moves = [
        (z_hbm, z_ref), (basis_hbm, basis_ref), (site_hbm, site_ref), (xy_hbm, xy_ref),
        (count_hbm, count_ref), (diag_hbm, diag_ref), (value_hbm, value_ref), (inv_hbm, own_rows),
    ]
    loads = [pltpu.make_async_copy(src, dst, in_sem.at[i]) for i, (src, dst) in enumerate(moves)]
    for load in loads:
        load.start()
    barrier = pltpu.get_barrier_semaphore()

    def greet(leaf, obs):
        pl.semaphore_signal(barrier, inc=1, device_id=(leaf, obs), device_id_type=MESH)

    partners(lambda level, q: greet(q, o))
    peers(lambda g: greet(p, g))

    def to_leaf(src, dst, send, recv, q, who):
        return pltpu.make_async_remote_copy(
            src_ref=src, dst_ref=dst, send_sem=send.at[q], recv_sem=recv.at[who],
            device_id=(q, o), device_id_type=MESH,
        )

    def a_copy(level, q, who):
        return to_leaf(proj.at[level], abuf.at[who], a_send, a_recv, q, who)

    def m_copy(q, who):
        return to_leaf(mbuf.at[who], mbuf.at[who], m_send, m_recv, q, who)

    def r_copy(q, who):
        part = rbuf.at[:, at(who * slots, slots)]
        return to_leaf(part, part, r_send, r_recv, q, who)

    def c_copy(q, who):
        return to_leaf(cbuf.at[who], cbuf.at[who], c_send, c_recv, q, who)

    def i_copy(g, who):
        part = ibuf.at[at(who * rows, rows), :]
        return pltpu.make_async_remote_copy(
            src_ref=inv_hbm, dst_ref=part, send_sem=i_send.at[g], recv_sem=i_recv.at[who],
            device_id=(p, g), device_id_type=MESH,
        )

    loads[0].wait()
    loads[1].wait()
    z = z_ref[...]
    for level in range(levels):
        proj[level] = dot_nt(z, basis_ref[level])

    pl.semaphore_wait(barrier, leaves - 1 + groups - 1)
    partners(lambda level, q: a_copy(level, q, p).start())
    peers(lambda g: i_copy(g, o).start())

    for load in loads[2:5]:
        load.wait()
    pick = (lax.broadcasted_iota(jnp.int32, (sites, slots), 0) == site_ref[...]).astype(jnp.float32)
    pick = pick.astype(jnp.bfloat16)
    row = lax.broadcasted_iota(jnp.int32, (MSG, sites), 0)
    coord = jnp.where(row < 3, xy_ref[0:1, :], xy_ref[1:2, :])
    first = coord.astype(jnp.bfloat16).astype(jnp.float32)
    second = (coord - first).astype(jnp.bfloat16).astype(jnp.float32)
    third = coord - first - second
    part = jnp.where(row % 3 == 0, first, jnp.where(row % 3 == 1, second, third))
    part = jnp.where(row < 6, part, 0.0).astype(jnp.bfloat16)
    message = dot(part, pick)
    count = count_ref[0].astype(jnp.float32)
    message = jnp.where(lax.broadcasted_iota(jnp.int32, (MSG, slots), 0) == 6, count, message)
    mbuf[p] = message
    partners(lambda level, q: m_copy(q, p).start())
    for load in loads[5:]:
        load.wait()
    at_slots = value_ref[...] - dot(z, dot(diag_ref[...], pick).astype(jnp.bfloat16))
    picked = [dot(basis_ref[level], pick).astype(jnp.bfloat16) for level in range(levels)]
    field = dot(z, diag_ref[...])

    partners(lambda level, q: a_copy(level, q, q).wait_recv())
    coefs = []
    for level in range(levels):
        width = 2**level
        half = p // width
        start = (half + 1 - 2 * (half % 2)) * width
        sums = abuf[start]
        if width <= UNROLL:
            for i in range(1, width):
                sums = sums + abuf[start + i]
        else:
            sums = lax.fori_loop(1, width, lambda i, s, start=start: s + abuf[start + i], sums)
        coefs.append(stacked(sums * (0.5 / (rank * width * sites) ** 0.5)))
    low = dot(coefs[0], picked[0])
    for level in range(1, levels):
        low = low + dot(coefs[level], picked[level])
    rbuf[:, at(p * slots, slots)] = at_slots - (low[:samples] + low[samples:])
    partners(lambda level, q: r_copy(q, p).start())

    partners(lambda level, q: m_copy(q, q).wait_recv())
    counts = jnp.concatenate([mbuf[q, 6:7, :] for q in range(leaves)], axis=0)
    below = lax.broadcasted_iota(jnp.int32, (leaves, leaves), 1) < lax.broadcasted_iota(
        jnp.int32, (leaves, leaves), 0
    )
    base = dot(below.astype(jnp.float32).astype(jnp.bfloat16), counts.astype(jnp.bfloat16))
    lane = lax.broadcasted_iota(jnp.int32, (leaves, slots), 1).astype(jnp.float32)
    slot_of[...] = jnp.where(lane < counts, base + lane, -1.0)
    chunk = min(CHUNK, total)
    number = lax.broadcasted_iota(jnp.int32, (chunk, slots), 0).astype(jnp.float32)
    peers(lambda g: i_copy(g, g).wait_recv())

    def one_chunk(c):
        inverse = stacked(ibuf[:, at(c * chunk, chunk)])
        shift = number + jnp.float32(c * chunk) if isinstance(c, int) else number + (c * chunk).astype(jnp.float32)

        def one_leaf(q):
            here = jnp.where(shift == slot_of[pl.ds(q, 1), :], 1.0, 0.0).astype(jnp.bfloat16)
            wide = dot(inverse, here)
            wide = wide[:owned] + wide[owned:]
            lanes = at(q * slots, slots)
            if chunk == total:
                xbuf[:, lanes] = wide
            else:
                xbuf[:, lanes] += wide
            places = dot_nt(here, mbuf[q].astype(jnp.bfloat16))
            lines = at(c * chunk, chunk)
            if isinstance(q, int) and q == 0:
                sbuf[lines, :] = places
            else:
                sbuf[lines, :] += places

        loop(leaves, one_leaf)

    if leaves > UNROLL:
        sbuf[...] = jnp.zeros_like(sbuf)
    if chunk < total:
        xbuf[...] = jnp.zeros_like(xbuf)
    loop(total // chunk, one_chunk)
    xh, xl = split(xbuf[...])

    partners(lambda level, q: r_copy(q, q).wait_recv())
    rh, rl = split(rbuf[...])
    both = dot_nt(jnp.concatenate([rh, rl], axis=0), xh)
    cbuf[p] = both[:samples] + both[samples:] + dot_nt(rh, xl)
    partners(lambda level, q: c_copy(q, p).start())

    low = dot(coefs[0], basis_ref[0])
    for level in range(1, levels):
        low = low + dot(coefs[level], basis_ref[level])
    out_ref[...] = field + (low[:samples] + low[samples:])

    def one_tile(c):
        lines = at(c * chunk, chunk)
        places = sbuf[lines, :]

        def column(i):
            return jnp.broadcast_to(places[:, i : i + 1], (chunk, sites))

        delta_x = (column(0) + column(1) + column(2)) - xy_ref[0:1, :]
        delta_y = (column(3) + column(4) + column(5)) - xy_ref[1:2, :]
        distance = jnp.sqrt(delta_x * delta_x + delta_y * delta_y)
        kh[lines, :], kl[lines, :] = split(jnp.exp(distance * (-1.0 / corr_length)))

    loop(total // chunk, one_tile)

    def drain(level, q):
        a_copy(level, q, p).wait_send()
        m_copy(q, p).wait_send()
        r_copy(q, p).wait_send()

    partners(drain)
    peers(lambda g: i_copy(g, o).wait_send())
    partners(lambda level, q: c_copy(q, q).wait_recv())

    def correct(q):
        coef = stacked(cbuf[q])
        lines = at(q * owned, owned)
        twice = dot(coef, kh[lines, :])
        return twice[:samples] + twice[samples:] + dot(coef[:samples], kl[lines, :])

    if leaves <= UNROLL:
        total_sum = correct(0)
        for q in range(1, leaves):
            total_sum = total_sum + correct(q)
    else:
        total_sum = lax.fori_loop(1, leaves, lambda q, s: s + correct(q), correct(0))
    out_ref[...] += total_sum
    partners(lambda level, q: c_copy(q, p).wait_send())


def body(samples_z, diag_block, level_basis, site_xy, obs_site, obs_value, obs_count, inverse_rows):
    leaves = lax.axis_size("leaf")
    groups = lax.axis_size("obs")
    samples, sites = samples_z.shape
    levels, rank, _ = level_basis.shape
    slots = obs_site.shape[0]
    rows, total = inverse_rows.shape
    owned = rows * groups
    vmem = pl.BlockSpec(memory_space=pltpu.VMEM)
    hbm = pl.BlockSpec(memory_space=pltpu.HBM)
    f32, bf16 = jnp.float32, jnp.bfloat16
    leaf_sem = pltpu.SemaphoreType.DMA((leaves,))
    obs_sem = pltpu.SemaphoreType.DMA((groups,))
    return pl.pallas_call(
        functools.partial(kernel, leaves, groups),
        out_shape=jax.ShapeDtypeStruct((samples, sites), f32),
        in_specs=[hbm] * 8,
        out_specs=vmem,
        scratch_shapes=[
            pltpu.VMEM(samples_z.shape, bf16),
            pltpu.VMEM(diag_block.shape, bf16),
            pltpu.VMEM(level_basis.shape, bf16),
            pltpu.VMEM(site_xy.shape, f32),
            pltpu.VMEM((1, slots), jnp.int32),
            pltpu.VMEM((1, slots), f32),
            pltpu.SMEM((1,), jnp.int32),
            pltpu.SemaphoreType.DMA((8,)),
            pltpu.VMEM((levels, samples, rank), f32),
            pltpu.VMEM((leaves, samples, rank), f32),
            pltpu.VMEM((leaves, MSG, slots), f32),
            pltpu.VMEM((owned, total), f32),
            pltpu.VMEM((samples, leaves * slots), f32),
            pltpu.VMEM((leaves, samples, owned), f32),
            pltpu.VMEM((owned, leaves * slots), f32),
            pltpu.VMEM((total, MSG), f32),
            pltpu.VMEM((total, sites), bf16),
            pltpu.VMEM((total, sites), bf16),
            pltpu.VMEM((leaves, slots), f32),
            leaf_sem, leaf_sem, leaf_sem, leaf_sem,
            obs_sem, obs_sem,
            leaf_sem, leaf_sem, leaf_sem, leaf_sem,
        ],
        compiler_params=pltpu.CompilerParams(
            collective_id=0, has_side_effects=True, vmem_limit_bytes=40 * 2**20
        ),
        cost_estimate=pl.CostEstimate(
            flops=2 * samples * sites * total * 4,
            bytes_accessed=4 * owned * total,
            transcendentals=2 * total * sites,
        ),
    )(
        samples_z,
        diag_block,
        level_basis,
        site_xy,
        obs_site.reshape(1, slots),
        obs_value.reshape(1, slots),
        obs_count,
        inverse_rows,
    )


def solution(mesh):
    in_specs = (
        P("obs", "leaf"),
        P("leaf", None),
        P(None, None, "leaf"),
        P(None, "leaf"),
        P("leaf"),
        P("leaf"),
        P("leaf"),
        P(("leaf", "obs"), None),
    )
    out_specs = P("obs", "leaf")
    return jax.shard_map(body, mesh=mesh, in_specs=in_specs, out_specs=out_specs, check_vma=False)
```

```python
import functools

import jax
import jax.numpy as jnp
from jax import lax
from jax.experimental import pallas as pl
from jax.experimental.pallas import tpu as pltpu
from jax.sharding import PartitionSpec as P

corr_length = 0.15
MESH = pl.DeviceIdType.MESH
NT = (((1,), (1,)), ((), ()))
UNROLL = 8
CHUNK = 512
MSG = 16


def dot(a, b):
    return jnp.dot(a, b, preferred_element_type=jnp.float32)


def dot_nt(a, b):
    return lax.dot_general(a, b, NT, preferred_element_type=jnp.float32)


def split(a):
    high = a.astype(jnp.bfloat16)
    return high, (a - high.astype(jnp.float32)).astype(jnp.bfloat16)


def stacked(a):
    high, low = split(a)
    return jnp.concatenate([high, low], axis=0)


def loop(count, step):
    if count <= UNROLL:
        for i in range(count):
            step(i)
    else:

        def one(i, carry):
            step(i)
            return carry

        lax.fori_loop(0, count, one, 0)


def at(start, size):
    start = start if isinstance(start, int) else pl.multiple_of(start, size)
    return pl.ds(start, size)


def kernel(
    leaves,
    groups,
    z_hbm,
    diag_hbm,
    basis_hbm,
    xy_hbm,
    site_hbm,
    value_hbm,
    count_hbm,
    inv_hbm,
    out_ref,
    z_ref,
    diag_ref,
    basis_ref,
    xy_ref,
    site_ref,
    value_ref,
    count_ref,
    in_sem,
    proj,
    abuf,
    mbuf,
    ibuf,
    rbuf,
    cbuf,
    xbuf,
    xt,
    sbuf,
    kh,
    kl,
    slot_of,
    a_send,
    a_recv,
    m_send,
    m_recv,
    i_send,
    i_recv,
    r_send,
    r_recv,
    c_send,
    c_recv,
):
    p = lax.axis_index("leaf")
    o = lax.axis_index("obs")
    levels, rank, sites = basis_ref.shape
    samples = z_ref.shape[0]
    slots = site_ref.shape[1]
    rows, total = inv_hbm.shape
    owned = rows * groups
    pack = max(1, min(leaves, 128 // owned))
    depth = levels * rank
    side = max(1, 128 // rank)
    tile = side * rank

    def partners(step):
        for level in reversed(range(levels)):
            width = 2**level
            half = p // width
            start = (half + 1 - 2 * (half % 2)) * width
            loop(width, functools.partial(lambda level, start, i: step(level, start + i), level, start))

    def peers(step):
        for e in range(1, groups):
            step((o + e) % groups)

    own_rows = ibuf.at[at(o * rows, rows), :]
    moves = [
        (z_hbm, z_ref), (basis_hbm, basis_ref), (site_hbm, site_ref), (xy_hbm, xy_ref),
        (count_hbm, count_ref), (diag_hbm, diag_ref), (value_hbm, value_ref), (inv_hbm, own_rows),
    ]
    loads = [pltpu.make_async_copy(src, dst, in_sem.at[i]) for i, (src, dst) in enumerate(moves)]
    for load in loads:
        load.start()
    barrier = pltpu.get_barrier_semaphore()

    def greet(leaf, obs):
        pl.semaphore_signal(barrier, inc=1, device_id=(leaf, obs), device_id_type=MESH)

    partners(lambda level, q: greet(q, o))
    peers(lambda g: greet(p, g))

    def to_leaf(src, dst, send, recv, q, who):
        return pltpu.make_async_remote_copy(
            src_ref=src, dst_ref=dst, send_sem=send.at[q], recv_sem=recv.at[who],
            device_id=(q, o), device_id_type=MESH,
        )

    def a_copy(level, q, who):
        return to_leaf(proj.at[level // side], abuf.at[who], a_send, a_recv, q, who)

    def m_copy(q, who):
        return to_leaf(mbuf.at[who], mbuf.at[who], m_send, m_recv, q, who)

    def r_copy(q, who):
        part = rbuf.at[:, at(who * slots, slots)]
        return to_leaf(part, part, r_send, r_recv, q, who)

    def c_copy(q, who):
        return to_leaf(cbuf.at[who], cbuf.at[who], c_send, c_recv, q, who)

    def i_copy(g, who):
        part = ibuf.at[at(who * rows, rows), :]
        return pltpu.make_async_remote_copy(
            src_ref=inv_hbm, dst_ref=part, send_sem=i_send.at[g], recv_sem=i_recv.at[who],
            device_id=(p, g), device_id_type=MESH,
        )

    loads[0].wait()
    loads[1].wait()
    z = z_ref[...]
    basis = basis_ref[...].reshape(depth, sites)
    project = dot_nt(z, basis)
    spare = proj.shape[0] * tile - depth
    if spare:
        project = jnp.concatenate([project, jnp.zeros((samples, spare), jnp.float32)], axis=1)
    for i in range(proj.shape[0]):
        proj[i] = project[:, i * tile : (i + 1) * tile]

    pl.semaphore_wait(barrier, leaves - 1 + groups - 1)
    partners(lambda level, q: a_copy(level, q, p).start())
    peers(lambda g: i_copy(g, o).start())

    for load in loads[2:5]:
        load.wait()
    pick = (lax.broadcasted_iota(jnp.int32, (sites, slots), 0) == site_ref[...]).astype(jnp.float32)
    pick = pick.astype(jnp.bfloat16)
    row = lax.broadcasted_iota(jnp.int32, (MSG, sites), 0)
    coord = jnp.where(row < 3, xy_ref[0:1, :], xy_ref[1:2, :])
    first = coord.astype(jnp.bfloat16).astype(jnp.float32)
    second = (coord - first).astype(jnp.bfloat16).astype(jnp.float32)
    third = coord - first - second
    part = jnp.where(row % 3 == 0, first, jnp.where(row % 3 == 1, second, third))
    part = jnp.where(row < 6, part, 0.0).astype(jnp.bfloat16)
    message = dot(part, pick)
    count = count_ref[0].astype(jnp.float32)
    message = jnp.where(lax.broadcasted_iota(jnp.int32, (MSG, slots), 0) == 6, count, message)
    mbuf[p] = message
    partners(lambda level, q: m_copy(q, p).start())
    for load in loads[5:]:
        load.wait()
    at_slots = value_ref[...] - dot(z, dot(diag_ref[...], pick).astype(jnp.bfloat16))
    picked = dot(basis, pick).astype(jnp.bfloat16)
    field = dot(z, diag_ref[...])

    partners(lambda level, q: a_copy(level, q, q).wait_recv())
    coefs = [jnp.zeros((samples, tile), jnp.float32)] * proj.shape[0]
    part_of = lax.broadcasted_iota(jnp.int32, (samples, tile), 1) // rank
    for level in range(levels):
        width = 2**level
        half = p // width
        start = (half + 1 - 2 * (half % 2)) * width
        sums = abuf[start]
        if width <= UNROLL:
            for i in range(1, width):
                sums = sums + abuf[start + i]
        else:
            sums = lax.fori_loop(1, width, lambda i, s, start=start: s + abuf[start + i], sums)
        sums = sums * (0.5 / (rank * width * sites) ** 0.5)
        coefs[level // side] = jnp.where(part_of == level % side, sums, coefs[level // side])
    coefs = stacked(jnp.concatenate(coefs, axis=1)[:, :depth])
    low = dot(coefs, picked)
    rbuf[:, at(p * slots, slots)] = at_slots - (low[:samples] + low[samples:])
    partners(lambda level, q: r_copy(q, p).start())

    partners(lambda level, q: m_copy(q, q).wait_recv())
    counts = jnp.concatenate([mbuf[q, 6:7, :] for q in range(leaves)], axis=0)
    below = lax.broadcasted_iota(jnp.int32, (leaves, leaves), 1) < lax.broadcasted_iota(
        jnp.int32, (leaves, leaves), 0
    )
    base = dot(below.astype(jnp.float32).astype(jnp.bfloat16), counts.astype(jnp.bfloat16))
    lane = lax.broadcasted_iota(jnp.int32, (leaves, slots), 1).astype(jnp.float32)
    slot_of[...] = jnp.where(lane < counts, base + lane, -1.0)
    chunk = min(CHUNK, total)
    number = lax.broadcasted_iota(jnp.int32, (chunk, slots), 0).astype(jnp.float32)
    peers(lambda g: i_copy(g, g).wait_recv())

    def one_chunk(c):
        inverse = stacked(ibuf[:, at(c * chunk, chunk)])
        shift = number + jnp.float32(c * chunk) if isinstance(c, int) else number + (c * chunk).astype(jnp.float32)

        def one_leaf(q):
            here = jnp.where(shift == slot_of[pl.ds(q, 1), :], 1.0, 0.0).astype(jnp.bfloat16)
            wide = dot(inverse, here)
            wide = wide[:owned] + wide[owned:]
            lanes = at(q * slots, slots)
            if chunk == total:
                xbuf[:, lanes] = wide
            else:
                xbuf[:, lanes] += wide
            places = dot_nt(here, mbuf[q].astype(jnp.bfloat16))
            lines = at(c * chunk, chunk)
            if isinstance(q, int) and q == 0:
                sbuf[lines, :] = places
            else:
                sbuf[lines, :] += places

        loop(leaves, one_leaf)

    if leaves > UNROLL:
        sbuf[...] = jnp.zeros_like(sbuf)
    if chunk < total:
        xbuf[...] = jnp.zeros_like(xbuf)
    loop(total // chunk, one_chunk)
    xh, xl = split(xbuf[...].T)
    lane = lax.broadcasted_iota(jnp.int32, (samples, pack * owned), 1)
    mine = lane // owned == p % pack
    xt[...] = jnp.concatenate([xh] * pack + [xl] * pack, axis=1)

    partners(lambda level, q: r_copy(q, q).wait_recv())
    rh, rl = split(rbuf[...])
    both = dot(jnp.concatenate([rh, rl], axis=0), xt[...])
    wide = pack * owned
    mixed = both[:samples, :wide] + both[samples:, :wide] + both[:samples, wide:]
    cbuf[p] = jnp.where(mine, mixed, 0.0)
    partners(lambda level, q: c_copy(q, p).start())

    low = dot(coefs, basis)
    out_ref[...] = field + (low[:samples] + low[samples:])

    def one_tile(c):
        lines = at(c * chunk, chunk)
        places = sbuf[lines, :]

        def column(i):
            return jnp.broadcast_to(places[:, i : i + 1], (chunk, sites))

        delta_x = (column(0) + column(1) + column(2)) - xy_ref[0:1, :]
        delta_y = (column(3) + column(4) + column(5)) - xy_ref[1:2, :]
        distance = jnp.sqrt(delta_x * delta_x + delta_y * delta_y)
        kh[lines, :], kl[lines, :] = split(jnp.exp(distance * (-1.0 / corr_length)))

    loop(total // chunk, one_tile)

    def drain(level, q):
        a_copy(level, q, p).wait_send()
        m_copy(q, p).wait_send()
        r_copy(q, p).wait_send()

    partners(drain)
    peers(lambda g: i_copy(g, o).wait_send())
    partners(lambda level, q: c_copy(q, q).wait_recv())

    shares = []
    for first_leaf in range(0, leaves, pack):
        share = cbuf[first_leaf]
        for q in range(first_leaf + 1, first_leaf + pack):
            share = share + cbuf[q]
        shares.append(share)
    ch, cl = split(jnp.concatenate(shares, axis=1))
    twice = dot(jnp.concatenate([ch, cl], axis=0), kh[...])
    out_ref[...] += twice[:samples] + twice[samples:] + dot(ch, kl[...])
    partners(lambda level, q: c_copy(q, p).wait_send())


def body(samples_z, diag_block, level_basis, site_xy, obs_site, obs_value, obs_count, inverse_rows):
    leaves = lax.axis_size("leaf")
    groups = lax.axis_size("obs")
    samples, sites = samples_z.shape
    levels, rank, _ = level_basis.shape
    slots = obs_site.shape[0]
    rows, total = inverse_rows.shape
    owned = rows * groups
    pack = max(1, min(leaves, 128 // owned))
    tile = max(1, 128 // rank) * rank
    tiles = pl.cdiv(levels * rank, tile)
    vmem = pl.BlockSpec(memory_space=pltpu.VMEM)
    hbm = pl.BlockSpec(memory_space=pltpu.HBM)
    f32, bf16 = jnp.float32, jnp.bfloat16
    leaf_sem = pltpu.SemaphoreType.DMA((leaves,))
    obs_sem = pltpu.SemaphoreType.DMA((groups,))
    return pl.pallas_call(
        functools.partial(kernel, leaves, groups),
        out_shape=jax.ShapeDtypeStruct((samples, sites), f32),
        in_specs=[hbm] * 8,
        out_specs=vmem,
        scratch_shapes=[
            pltpu.VMEM(samples_z.shape, bf16),
            pltpu.VMEM(diag_block.shape, bf16),
            pltpu.VMEM(level_basis.shape, bf16),
            pltpu.VMEM(site_xy.shape, f32),
            pltpu.VMEM((1, slots), jnp.int32),
            pltpu.VMEM((1, slots), f32),
            pltpu.SMEM((1,), jnp.int32),
            pltpu.SemaphoreType.DMA((8,)),
            pltpu.VMEM((tiles, samples, tile), f32),
            pltpu.VMEM((leaves, samples, tile), f32),
            pltpu.VMEM((leaves, MSG, slots), f32),
            pltpu.VMEM((owned, total), f32),
            pltpu.VMEM((samples, leaves * slots), f32),
            pltpu.VMEM((leaves, samples, pack * owned), f32),
            pltpu.VMEM((owned, leaves * slots), f32),
            pltpu.VMEM((leaves * slots, 2 * pack * owned), bf16),
            pltpu.VMEM((total, MSG), f32),
            pltpu.VMEM((total, sites), bf16),
            pltpu.VMEM((total, sites), bf16),
            pltpu.VMEM((leaves, slots), f32),
            leaf_sem, leaf_sem, leaf_sem, leaf_sem,
            obs_sem, obs_sem,
            leaf_sem, leaf_sem, leaf_sem, leaf_sem,
        ],
        compiler_params=pltpu.CompilerParams(
            collective_id=0, has_side_effects=True, vmem_limit_bytes=62 * 2**20
        ),
        cost_estimate=pl.CostEstimate(
            flops=2 * samples * sites * total * 4,
            bytes_accessed=4 * owned * total,
            transcendentals=2 * total * sites,
        ),
    )(
        samples_z,
        diag_block,
        level_basis,
        site_xy,
        obs_site.reshape(1, slots),
        obs_value.reshape(1, slots),
        obs_count,
        inverse_rows,
    )


def solution(mesh):
    in_specs = (
        P("obs", "leaf"),
        P("leaf", None),
        P(None, None, "leaf"),
        P(None, "leaf"),
        P("leaf"),
        P("leaf"),
        P("leaf"),
        P(("leaf", "obs"), None),
    )
    out_specs = P("obs", "leaf")
    return jax.shard_map(body, mesh=mesh, in_specs=in_specs, out_specs=out_specs, check_vma=False)
```

```python
import functools

import jax
import jax.numpy as jnp
from jax import lax
from jax.experimental import pallas as pl
from jax.experimental.pallas import tpu as pltpu
from jax.sharding import PartitionSpec as P

corr_length = 0.15
MESH = pl.DeviceIdType.MESH
NT = (((1,), (1,)), ((), ()))
UNROLL = 8
CHUNK = 512
MSG = 16


def dot(a, b):
    return jnp.dot(a, b, preferred_element_type=jnp.float32)


def dot_nt(a, b):
    return lax.dot_general(a, b, NT, preferred_element_type=jnp.float32)


def split(a):
    high = a.astype(jnp.bfloat16)
    return high, (a - high.astype(jnp.float32)).astype(jnp.bfloat16)


def stacked(a):
    high, low = split(a)
    return jnp.concatenate([high, low], axis=0)


def thirds(x, y):
    row = lax.broadcasted_iota(jnp.int32, (MSG, x.shape[1]), 0)
    coord = jnp.where(row < 3, x, y)
    first = coord.astype(jnp.bfloat16).astype(jnp.float32)
    second = (coord - first).astype(jnp.bfloat16).astype(jnp.float32)
    part = jnp.where(row % 3 == 0, first, jnp.where(row % 3 == 1, second, coord - first - second))
    return jnp.where(row < 6, part, 0.0).astype(jnp.bfloat16)


def fold(twin):
    half = twin.shape[0] // 2
    left = lax.broadcasted_iota(jnp.int32, (half, twin.shape[1]), 1) < twin.shape[1] // 2
    return jnp.where(left, twin[:half], twin[half:])


def unfold(even, odd):
    middle = even.shape[1] // 2
    left = lax.broadcasted_iota(jnp.int32, even.shape, 1) < middle
    upper = jnp.where(left, even, pltpu.roll(odd, middle, 1))
    lower = jnp.where(left, pltpu.roll(even, middle, 1), odd)
    return jnp.concatenate([upper, lower], axis=0)


def loop(count, step):
    if count <= UNROLL:
        for i in range(count):
            step(i)
    else:

        def one(i, carry):
            step(i)
            return carry

        lax.fori_loop(0, count, one, 0)


def at(start, size):
    start = start if isinstance(start, int) else pl.multiple_of(start, size)
    return pl.ds(start, size)


def kernel(
    leaves,
    groups,
    z_hbm,
    diag_hbm,
    basis_hbm,
    xy_hbm,
    site_hbm,
    value_hbm,
    count_hbm,
    inv_hbm,
    out_ref,
    z_ref,
    diag_ref,
    basis_ref,
    xy_ref,
    site_ref,
    value_ref,
    count_ref,
    in_sem,
    proj,
    abuf,
    mbuf,
    ibuf,
    rbuf,
    cbuf,
    xbuf,
    xt,
    sbuf,
    kh,
    kl,
    slot_of,
    a_send,
    a_recv,
    m_send,
    m_recv,
    i_send,
    i_recv,
    r_send,
    r_recv,
    c_send,
    c_recv,
):
    p = lax.axis_index("leaf")
    o = lax.axis_index("obs")
    levels, rank, sites = basis_ref.shape
    samples = z_ref.shape[0]
    slots = site_ref.shape[1]
    rows, total = inv_hbm.shape
    owned = rows * groups
    depth = levels * rank

    def partners(step):
        for level in reversed(range(levels)):
            width = 2**level
            half = p // width
            start = (half + 1 - 2 * (half % 2)) * width
            loop(width, functools.partial(lambda level, start, i: step(level, start + i), level, start))

    def peers(step):
        for e in range(1, groups):
            step((o + e) % groups)

    own_rows = ibuf.at[at(o * rows, rows), :]
    moves = [
        (z_hbm, z_ref), (basis_hbm, basis_ref), (site_hbm, site_ref), (xy_hbm, xy_ref),
        (count_hbm, count_ref), (diag_hbm, diag_ref), (value_hbm, value_ref), (inv_hbm, own_rows),
    ]
    loads = [pltpu.make_async_copy(src, dst, in_sem.at[i]) for i, (src, dst) in enumerate(moves)]
    for load in loads:
        load.start()
    barrier = pltpu.get_barrier_semaphore()

    def greet(leaf, obs):
        pl.semaphore_signal(barrier, inc=1, device_id=(leaf, obs), device_id_type=MESH)

    partners(lambda level, q: greet(q, o))
    peers(lambda g: greet(p, g))

    def to_leaf(src, dst, send, recv, q, who):
        return pltpu.make_async_remote_copy(
            src_ref=src, dst_ref=dst, send_sem=send.at[q], recv_sem=recv.at[who],
            device_id=(q, o), device_id_type=MESH,
        )

    def a_copy(level, q, who):
        return to_leaf(proj.at[level], abuf.at[who], a_send, a_recv, q, who)

    def m_copy(q, who):
        return to_leaf(mbuf.at[who], mbuf.at[who], m_send, m_recv, q, who)

    def r_copy(q, who):
        return to_leaf(rbuf.at[who], rbuf.at[who], r_send, r_recv, q, who)

    def c_copy(q, who):
        return to_leaf(cbuf.at[who], cbuf.at[who], c_send, c_recv, q, who)

    def i_copy(g, who):
        part = ibuf.at[at(who * rows, rows), :]
        return pltpu.make_async_remote_copy(
            src_ref=inv_hbm, dst_ref=part, send_sem=i_send.at[g], recv_sem=i_recv.at[who],
            device_id=(p, g), device_id_type=MESH,
        )

    loads[0].wait()
    loads[1].wait()
    z = z_ref[...]
    basis = basis_ref[...].reshape(depth, sites)
    twins = [basis_ref[level // 2] for level in range(2 * levels)]
    project = dot_nt(z, jnp.concatenate(twins, axis=0))
    for level in range(levels):
        proj[level] = fold(project[:, level * 2 * rank : (level + 1) * 2 * rank])

    pl.semaphore_wait(barrier, leaves - 1 + groups - 1)
    partners(lambda level, q: a_copy(level, q, p).start())
    peers(lambda g: i_copy(g, o).start())

    for load in loads[2:5]:
        load.wait()
    pick = (lax.broadcasted_iota(jnp.int32, (sites, slots), 0) == site_ref[...]).astype(jnp.float32)
    pick = pick.astype(jnp.bfloat16)
    part = thirds(xy_ref[0:1, :], xy_ref[1:2, :])
    message = dot(part, pick)
    count = count_ref[0].astype(jnp.float32)
    mbuf[p, :, :slots] = message[0:1] + message[1:2] + message[2:3]
    mbuf[p, :, slots : 2 * slots] = message[3:4] + message[4:5] + message[5:6]
    mbuf[p, :, 2 * slots :] = jnp.full((1, slots), count)
    partners(lambda level, q: m_copy(q, p).start())
    for load in loads[5:]:
        load.wait()
    at_slots = value_ref[...] - dot(z, dot(diag_ref[...], pick).astype(jnp.bfloat16))
    picked = dot(basis, pick).astype(jnp.bfloat16)
    field = dot(z, diag_ref[...])

    partners(lambda level, q: a_copy(level, q, q).wait_recv())
    coefs = []
    for level in range(levels):
        width = 2**level
        half = p // width
        start = (half + 1 - 2 * (half % 2)) * width
        sums = abuf[start]
        if width <= UNROLL:
            for i in range(1, width):
                sums = sums + abuf[start + i]
        else:
            sums = lax.fori_loop(1, width, lambda i, s, start=start: s + abuf[start + i], sums)
        coefs.append(sums * (0.5 / (rank * width * sites) ** 0.5))
    coefs = coefs + coefs[-1:] * (levels % 2)
    coefs = [unfold(coefs[i], coefs[i + 1]) for i in range(0, len(coefs), 2)]
    coefs = stacked(jnp.concatenate(coefs, axis=1)[:, :depth])
    low = dot(coefs, picked)
    rbuf[p] = at_slots - (low[:samples] + low[samples:])
    partners(lambda level, q: r_copy(q, p).start())

    partners(lambda level, q: m_copy(q, q).wait_recv())
    counts = jnp.concatenate([mbuf[q, :, 2 * slots :] for q in range(leaves)], axis=0)
    below = lax.broadcasted_iota(jnp.int32, (leaves, leaves), 1) < lax.broadcasted_iota(
        jnp.int32, (leaves, leaves), 0
    )
    base = dot(below.astype(jnp.float32).astype(jnp.bfloat16), counts.astype(jnp.bfloat16))
    lane = lax.broadcasted_iota(jnp.int32, (leaves, slots), 1).astype(jnp.float32)
    slot_of[...] = jnp.where(lane < counts, base + lane, -1.0)
    chunk = min(CHUNK, total)
    number = lax.broadcasted_iota(jnp.int32, (chunk, slots), 0).astype(jnp.float32)
    peers(lambda g: i_copy(g, g).wait_recv())

    def one_chunk(c):
        inverse = stacked(ibuf[:, at(c * chunk, chunk)])
        shift = number + jnp.float32(c * chunk) if isinstance(c, int) else number + (c * chunk).astype(jnp.float32)

        def one_leaf(q):
            here = jnp.where(shift == slot_of[pl.ds(q, 1), :], 1.0, 0.0).astype(jnp.bfloat16)
            wide = dot(inverse, here)
            wide = wide[:owned] + wide[owned:]
            lanes = at(q * slots, slots)
            if chunk == total:
                xbuf[:, lanes] = wide
            else:
                xbuf[:, lanes] += wide
            places = dot_nt(here, thirds(mbuf[q, :, :slots], mbuf[q, :, slots : 2 * slots]))
            lines = at(c * chunk, chunk)
            if isinstance(q, int) and q == 0:
                sbuf[lines, :] = places
            else:
                sbuf[lines, :] += places

        loop(leaves, one_leaf)

    if leaves > UNROLL:
        sbuf[...] = jnp.zeros_like(sbuf)
    if chunk < total:
        xbuf[...] = jnp.zeros_like(xbuf)
    loop(total // chunk, one_chunk)
    xh, xl = split(xbuf[...].T)
    xt[...] = jnp.concatenate([xh, xh, xl, xl], axis=1)

    partners(lambda level, q: r_copy(q, q).wait_recv())
    rh, rl = split(jnp.concatenate([rbuf[q] for q in range(leaves)], axis=1))
    both = dot(jnp.concatenate([rh, rl], axis=0), xt[...])
    wide = 2 * owned
    mixed = both[:samples, :wide] + both[samples:, :wide] + both[:samples, wide:]
    cbuf[p] = fold(mixed)
    partners(lambda level, q: c_copy(q, p).start())

    low = dot(coefs, basis)
    out_ref[...] = field + (low[:samples] + low[samples:])

    def one_tile(c):
        lines = at(c * chunk, chunk)
        places = sbuf[lines, :]

        def column(i):
            return jnp.broadcast_to(places[:, i : i + 1], (chunk, sites))

        delta_x = (column(0) + column(1) + column(2)) - xy_ref[0:1, :]
        delta_y = (column(3) + column(4) + column(5)) - xy_ref[1:2, :]
        distance = jnp.sqrt(delta_x * delta_x + delta_y * delta_y)
        kh[lines, :], kl[lines, :] = split(jnp.exp(distance * (-1.0 / corr_length)))

    loop(total // chunk, one_tile)

    def drain(level, q):
        a_copy(level, q, p).wait_send()
        m_copy(q, p).wait_send()
        r_copy(q, p).wait_send()

    partners(drain)
    peers(lambda g: i_copy(g, o).wait_send())
    partners(lambda level, q: c_copy(q, q).wait_recv())

    shares = [unfold(cbuf[q], cbuf[q + 1]) for q in range(0, leaves, 2)]
    ch, cl = split(jnp.concatenate(shares, axis=1))
    twice = dot(jnp.concatenate([ch, cl], axis=0), kh[...])
    out_ref[...] += twice[:samples] + twice[samples:] + dot(ch, kl[...])
    partners(lambda level, q: c_copy(q, p).wait_send())


def body(samples_z, diag_block, level_basis, site_xy, obs_site, obs_value, obs_count, inverse_rows):
    leaves = lax.axis_size("leaf")
    groups = lax.axis_size("obs")
    samples, sites = samples_z.shape
    levels, rank, _ = level_basis.shape
    slots = obs_site.shape[0]
    rows, total = inverse_rows.shape
    owned = rows * groups
    vmem = pl.BlockSpec(memory_space=pltpu.VMEM)
    hbm = pl.BlockSpec(memory_space=pltpu.HBM)
    f32, bf16 = jnp.float32, jnp.bfloat16
    leaf_sem = pltpu.SemaphoreType.DMA((leaves,))
    obs_sem = pltpu.SemaphoreType.DMA((groups,))
    return pl.pallas_call(
        functools.partial(kernel, leaves, groups),
        out_shape=jax.ShapeDtypeStruct((samples, sites), f32),
        in_specs=[hbm] * 8,
        out_specs=vmem,
        scratch_shapes=[
            pltpu.VMEM(samples_z.shape, bf16),
            pltpu.VMEM(diag_block.shape, bf16),
            pltpu.VMEM(level_basis.shape, bf16),
            pltpu.VMEM(site_xy.shape, f32),
            pltpu.VMEM((1, slots), jnp.int32),
            pltpu.VMEM((1, slots), f32),
            pltpu.SMEM((1,), jnp.int32),
            pltpu.SemaphoreType.DMA((8,)),
            pltpu.VMEM((levels, samples // 2, 2 * rank), f32),
            pltpu.VMEM((leaves, samples // 2, 2 * rank), f32),
            pltpu.VMEM((leaves, 1, 3 * slots), f32),
            pltpu.VMEM((owned, total), f32),
            pltpu.VMEM((leaves, samples, slots), f32),
            pltpu.VMEM((leaves, samples // 2, 2 * owned), f32),
            pltpu.VMEM((owned, leaves * slots), f32),
            pltpu.VMEM((leaves * slots, 4 * owned), bf16),
            pltpu.VMEM((total, MSG), f32),
            pltpu.VMEM((total, sites), bf16),
            pltpu.VMEM((total, sites), bf16),
            pltpu.VMEM((leaves, slots), f32),
            leaf_sem, leaf_sem, leaf_sem, leaf_sem,
            obs_sem, obs_sem,
            leaf_sem, leaf_sem, leaf_sem, leaf_sem,
        ],
        compiler_params=pltpu.CompilerParams(
            collective_id=0, has_side_effects=True, vmem_limit_bytes=62 * 2**20
        ),
        cost_estimate=pl.CostEstimate(
            flops=2 * samples * sites * total * 4,
            bytes_accessed=4 * owned * total,
            transcendentals=2 * total * sites,
        ),
    )(
        samples_z,
        diag_block,
        level_basis,
        site_xy,
        obs_site.reshape(1, slots),
        obs_value.reshape(1, slots),
        obs_count,
        inverse_rows,
    )


def solution(mesh):
    in_specs = (
        P("obs", "leaf"),
        P("leaf", None),
        P(None, None, "leaf"),
        P(None, "leaf"),
        P("leaf"),
        P("leaf"),
        P("leaf"),
        P(("leaf", "obs"), None),
    )
    out_specs = P("obs", "leaf")
    return jax.shard_map(body, mesh=mesh, in_specs=in_specs, out_specs=out_specs, check_vma=False)
```
